512 devices in a mesh: seq: 32 (over x, y, core), tp: 16 (over z).
Axes of the slice: x: 4, y: 4, z: 16, core: 2. Of those that a mesh axis runs over, the one named last changes fastest.
Arguments:
- gate_values: bfloat16 [3072, 28672], P('seq', 'tp'), may hold values from -6 to 6
- up_values: bfloat16 [3072, 28672], P('seq', 'tp'), may hold values from -6 to 6
- weight_codes: bfloat16 [28672, 8192], P('tp', 'seq'), may hold values from -127 to 127
- exponents: int32 [8192], P('seq'), may hold values from -15 to -13
- token_scale: float32 [3072], replicated, may hold values from 0.006 to 0.06
Outputs:
- layer_output: bfloat16 [3072, 8192], P('tp', 'seq')
The draws below stay inside these ranges and needn't reach their ends.
All inputs are finite; a program needn't handle non-finite values.
Results may differ from the reference program's by a relative error of at most 0.0048.
Values may be sent and summed in bfloat16 or wider, within the bound.
A program may use at most 64 MiB of HBM per device.

```python
import math
import jax
import jax.numpy as jnp
import numpy as np
from jax import lax

D = 8192
FF = 28672
TOKENS = 3072
POW = 1024


def draw_weight_codes(key, part):
    key = jax.random.fold_in(key, 7)
    values = jax.random.uniform(key, (FF, D), jnp.float32, -127.0, 128.0)
    return jnp.minimum(jnp.floor(values), 127.0).astype(jnp.bfloat16)


def place_ends(values, own_key, least, high):
    extent = values.shape
    spot = [jax.random.randint(jax.random.fold_in(own_key, axis), (), 0, extent[axis]) for axis in range(len(extent))]
    values = values.at[tuple(spot)].set(least)
    longest = extent.index(max(extent))
    spot[longest] = (spot[longest] + 1) % extent[longest]
    return values.at[tuple(spot)].set(high)


def shard_levels(rng, extent, pieces, least, largest):
    factor_of = 1.0
    for dim, blocks in pieces:
        heights = jax.random.uniform(jax.random.fold_in(jax.random.fold_in(rng, 6), dim), (blocks,), jnp.float32, least / len(pieces), largest / len(pieces))
        factor_of = factor_of * jnp.repeat(jnp.exp(heights), extent[dim] // blocks).reshape((-1,) + (1,) * (len(extent) - 1 - dim))
    return factor_of


def centred(rng, extent, deviation, most, cuts=(), held_as=jnp.bfloat16):
    factor_of = shard_levels(rng, extent, cuts, -0.22, 0.18) if cuts else 1.0
    drawn = jax.random.normal(rng, extent, jnp.float32) * deviation * factor_of
    return jnp.minimum(jnp.maximum(drawn, -most), most).astype(held_as)


def setup_inputs(seed: int = 0) -> dict:
    seeds = jax.random.split(jax.random.key(seed), 6)
    return {
        "gate_values": centred(seeds[0], (TOKENS, FF), 1.0, 6.0, ((0, 32), (1, 16))),
        "up_values": centred(seeds[1], (TOKENS, FF), 1.0, 6.0, ((0, 32), (1, 16))),
        "weight_codes": draw_weight_codes(jax.random.fold_in(seeds[5], 71), 0),
        "exponents": place_ends(jax.random.randint(seeds[3], (D,), -15, -12), jax.random.fold_in(seeds[3], 1), -15, (-12) - 1).astype(jnp.int32),
        "token_scale": jnp.clip(jnp.exp(jax.random.uniform(seeds[4], (TOKENS,), jnp.float32, math.log(0.006), math.log(0.06))), 0.006, 0.06),
    }


def paley_table():
    residues = [number * number % 13 for number in range(1, 13)]
    legendre = np.array([0.0] + [1.0 if number in residues else -1.0 for number in range(1, 13)])
    offsets = (np.arange(13)[None, :] - np.arange(13)[:, None]) % 13
    conference = np.zeros((14, 14))
    conference[0, 1:] = 1.0
    conference[1:, 0] = 1.0
    conference[1:, 1:] = legendre[offsets]
    upper_pair = np.array([[1.0, 1.0], [1.0, -1.0]])
    lower_pair = np.array([[1.0, -1.0], [-1.0, -1.0]])
    paley_matrix = np.kron(conference, upper_pair) + np.kron(np.eye(14), lower_pair)
    return jnp.asarray(paley_matrix, dtype=jnp.float32)

def sylvester(matrix_order):
    table = np.ones((1, 1))
    doubling = np.array([[1.0, 1.0], [1.0, -1.0]])
    for level in range(matrix_order.bit_length() - 1):
        table = np.kron(doubling, table)
    return jnp.asarray(table, dtype=jnp.float32)

def reference(gate_values, up_values, weight_codes, exponents, token_scale):
    hidden = jax.nn.silu(gate_values.astype(jnp.float32)) * up_values.astype(jnp.float32)
    blocked = hidden.reshape(TOKENS, POW, 28)
    paley_mixed = jnp.einsum('tce,ae->tca', blocked, paley_table(), precision=lax.Precision.HIGHEST)
    full_mixed = jnp.einsum('tca,bc->tba', paley_mixed, sylvester(POW), precision=lax.Precision.HIGHEST)
    rotated = full_mixed.reshape(TOKENS, FF) * (1.0 / math.sqrt(FF))
    quantized = jnp.clip(rotated / token_scale[:, None], -127.0, 127.0).astype(jnp.bfloat16)
    summed = jnp.dot(quantized, weight_codes, preferred_element_type=jnp.float32)
    scales = token_scale[:, None] * jnp.exp2(exponents.astype(jnp.float32))[None, :]
    return (summed * scales).astype(jnp.bfloat16)
```

```python
import functools, math
import jax, jax.numpy as jnp, numpy as np
from jax import lax
from jax.experimental import pallas as pl
from jax.experimental.pallas import tpu as pltpu
from jax.sharding import PartitionSpec as P
MESH = pl.DeviceIdType.MESH

def paley_table():
    residues = [number * number % 13 for number in range(1, 13)]
    legendre = np.array([0.0] + [1.0 if number in residues else -1.0 for number in range(1, 13)])
    offsets = (np.arange(13)[None, :] - np.arange(13)[:, None]) % 13
    conference = np.zeros((14, 14))
    conference[0, 1:] = 1.0
    conference[1:, 0] = 1.0
    conference[1:, 1:] = legendre[offsets]
    upper_pair = np.array([[1.0, 1.0], [1.0, -1.0]])
    lower_pair = np.array([[1.0, -1.0], [-1.0, -1.0]])
    return np.kron(conference, upper_pair) + np.kron(np.eye(14), lower_pair)

def sylvester(n):
    t = np.ones((1, 1))
    d = np.array([[1.0, 1.0], [1.0, -1.0]])
    for _ in range(n.bit_length() - 1):
        t = np.kron(d, t)
    return t

Z = 16
T = 14
ROWS = 96

def k1(gate_ref, up_ref, scale_ref, mix_ref, out_ref, send_buf, recv_buf, q_buf,
       send1, recv1, send2, recv2):
    z = lax.axis_index("tp")
    core = lax.rem(lax.axis_index("seq"), 2)
    barrier = pltpu.get_barrier_semaphore()
    for d in range(1, Z):
        pl.semaphore_signal(barrier, inc=1, device_id={"tp": lax.rem(z + d, Z)}, device_id_type=MESH)

    g = gate_ref[...].astype(jnp.float32)
    hidden = g / (1.0 + jnp.exp(-g)) * up_ref[...].astype(jnp.float32)
    hi = hidden.astype(jnp.bfloat16)
    lo = (hidden - hi.astype(jnp.float32)).astype(jnp.bfloat16)
    half = T * 128 // 2
    stacked = jnp.concatenate([hi[:, :half], hi[:, half:], lo[:, :half], lo[:, half:]], axis=0)
    mixed = jnp.dot(stacked, mix_ref[...], preferred_element_type=jnp.float32)
    first = mixed[:ROWS] + mixed[2 * ROWS:3 * ROWS]
    second = mixed[ROWS:2 * ROWS] + mixed[3 * ROWS:]
    plus = (first + second).astype(jnp.bfloat16)
    minus = (first - second).astype(jnp.bfloat16)
    for t in range(T // 2):
        send_buf[t] = plus[:, t * 128:(t + 1) * 128]
        send_buf[T // 2 + t] = minus[:, t * 128:(t + 1) * 128]
    pl.semaphore_wait(barrier, Z - 1)

    shift = 8 * core
    mine = lax.rem(z + Z - shift, Z)
    order = [8, 7, 9, 6, 10, 5, 11, 4, 12, 3, 13, 2, 14, 1, 15]

    def copy1(tile, slot, dest):
        return pltpu.make_async_remote_copy(
            src_ref=send_buf.at[tile], dst_ref=recv_buf.at[slot], send_sem=send1.at[tile],
            recv_sem=recv1.at[slot], device_id={"tp": dest}, device_id_type=MESH)

    def copy2(dest, tile):
        return pltpu.make_async_remote_copy(
            src_ref=q_buf.at[dest], dst_ref=out_ref.at[:, pl.ds(pl.multiple_of(tile * 128, 128), 128)],
            send_sem=send2.at[dest], recv_sem=recv2.at[tile], device_id={"tp": dest}, device_id_type=MESH)

    for d in order:
        dest = lax.rem(z + d, Z)
        tile = lax.rem(dest + Z - shift, Z)
        @pl.when(tile < T)
        def _():
            copy1(tile, z, dest).start()

    @pl.when(mine < T)
    def _():
        recv_buf[z] = send_buf[mine]
        for d in order:
            src = lax.rem(z + Z - d, Z)
            copy1(mine, src, src).wait_recv()
        def rows(r, c):
            sl = pl.ds(r * 16, 16)
            v = [recv_buf[i, sl, :].astype(jnp.float32) for i in range(Z)]
            step = 1
            while step < Z:
                nv = list(v)
                for i in range(Z):
                    if i & step == 0:
                        nv[i] = v[i] + v[i | step]
                        nv[i | step] = v[i] - v[i | step]
                v = nv
                step *= 2
            sc = scale_ref[sl, :]
            for i in range(Z):
                q_buf[i, sl, :] = jnp.clip(v[i] * sc, -127.0, 127.0).astype(jnp.bfloat16)
            return c
        lax.fori_loop(0, ROWS // 16, rows, 0)
        for d in order:
            dest = lax.rem(z + d, Z)
            copy2(dest, mine).start()
        out_ref[:, pl.ds(pl.multiple_of(mine * 128, 128), 128)] = q_buf[z]

    for d in order:
        src = lax.rem(z + Z - d, Z)
        tile = lax.rem(src + Z - shift, Z)
        @pl.when(tile < T)
        def _():
            copy2(src, tile).wait_recv()
            copy1(tile, z, src).wait_send()
    @pl.when(mine < T)
    def _():
        for d in order:
            copy2(lax.rem(z + d, Z), mine).wait_send()


def rotate(gate, up, scale):
    mix = jnp.asarray(np.kron(sylvester(32), paley_table()).T, jnp.bfloat16)
    v = pl.BlockSpec(memory_space=pltpu.VMEM)
    dma = pltpu.SemaphoreType.DMA
    buf = pltpu.VMEM((Z, ROWS, 128), jnp.bfloat16)
    return pl.pallas_call(
        k1, out_shape=jax.ShapeDtypeStruct((ROWS, T * 128), jnp.bfloat16),
        in_specs=[v] * 4, out_specs=v,
        scratch_shapes=[buf, buf, buf, dma((Z,)), dma((Z,)), dma((Z,)), dma((Z,))],
        compiler_params=pltpu.CompilerParams(collective_id=0, has_side_effects=True, vmem_limit_bytes=40 << 20),
    )(gate, up, scale, mix)


WIDE = 3

ORDER = [(0, 0), (1, 0), (3, 0), (0, 1), (0, 3), (2, 0), (0, 2), (1, 1), (3, 1), (1, 3), (3, 3),
         (2, 1), (2, 3), (1, 2), (3, 2), (2, 2)]
CLASS = [[0], [1, 2, 3, 4], [5, 6, 7, 8, 9, 10], [11, 12, 13, 14], [15]]


def packed(values):
    word = sum(v << (2 * i) for i, v in enumerate(values))
    return word - (1 << 32) if word >= 1 << 31 else word


def k2(q_ref, w_ref, row_ref, col_ref, out_ref, act, part, in16, in32, st16, st32,
       ag_recv, sib_recv, ag_send, rs_recv, rs_send):
    z = lax.axis_index("tp")
    seq = lax.axis_index("seq")
    core = lax.rem(seq, 2)
    x, y = seq // 8, lax.rem(seq // 2, 4)
    u = x * (1 - core) + y * core
    v = y * (1 - core) + x * core

    def place(uu, vv):
        return 8 * (uu * (1 - core) + vv * core) + 2 * (vv * (1 - core) + uu * core) + core

    def chip(du, dv):
        return place(lax.rem(u + du, 4), lax.rem(v + dv, 4)) // 2

    up_u, dn_u = place(lax.rem(u + 1, 4), v), place(lax.rem(u + 3, 4), v)
    up_v, dn_v = place(u, lax.rem(v + 1, 4)), place(u, lax.rem(v + 3, 4))
    sibling = seq + 1 - 2 * core
    up_z, dn_z = lax.rem(z + 1, Z), lax.rem(z + 15, Z)

    barrier = pltpu.get_barrier_semaphore()
    for peer in (up_u, dn_u, up_v, dn_v, sibling):
        pl.semaphore_signal(barrier, inc=1, device_id={"seq": peer}, device_id_type=MESH)
    for peer in (up_z, dn_z):
        pl.semaphore_signal(barrier, inc=1, device_id={"tp": peer}, device_id_type=MESH)
    for h in range(2):
        act[seq, h] = q_ref[pl.ds(48 * h, 48), :]
    pl.semaphore_wait(barrier, 7)

    def send(block, h, slot, peer):
        return pltpu.make_async_remote_copy(
            src_ref=act.at[block, h], dst_ref=act.at[block, h], send_sem=ag_send.at[block // 2, h, slot],
            recv_sem=ag_recv.at[block // 2, h], device_id={"seq": peer}, device_id_type=MESH)

    def to_sibling(block, h):
        return pltpu.make_async_remote_copy(
            src_ref=act.at[block, h], dst_ref=act.at[block, h], send_sem=ag_send.at[block // 2, h, 4],
            recv_sem=sib_recv.at[block // 2, h], device_id={"seq": sibling}, device_id_type=MESH)

    def rightward(bu, bv, h):
        return lax.rem(bu + bv + h, 2) == 0

    def starts(du, dv, h):
        bu, bv = lax.rem(u + du, 4), lax.rem(v + dv, 4)
        block = place(bu, bv)
        right = rightward(bu, bv, h)
        if dv == 0:
            if du == 0:
                yield send(block, h, 0, up_u), None
                yield send(block, h, 1, dn_u), None
            elif du == 3:
                yield send(block, h, 0, up_u), right
            elif du == 1:
                yield send(block, h, 1, dn_u), jnp.logical_not(right)
            yield send(block, h, 2, up_v), None
            yield send(block, h, 3, dn_v), None
        elif dv == 3:
            yield send(block, h, 2, up_v), right
        elif dv == 1:
            yield send(block, h, 3, dn_v), jnp.logical_not(right)
        yield to_sibling(block, h), None

    def run(du, dv, h, what):
        for copy, cond in starts(du, dv, h):
            if cond is None:
                getattr(copy, what)()
            else:
                pl.when(cond)(getattr(copy, what))

    def receive(classes):
        for h in range(2):
            for s in CLASS[classes]:
                du, dv = ORDER[s]
                block = place(lax.rem(u + du, 4), lax.rem(v + dv, 4))
                send(block, h, 0, seq).wait_recv()
                run(du, dv, h, "start")

    def chain(source, e, k, wide, rows):
        buf = (st32, in32) if wide else (st16, in16)
        return pltpu.make_async_remote_copy(
            src_ref=buf[0].at[k, rows], dst_ref=buf[1].at[e, k, rows], send_sem=rs_send.at[e, k],
            recv_sem=rs_recv.at[e, k], device_id={"tp": jnp.where(e == 0, up_z, dn_z)}, device_id_type=MESH)

    ALL, FIRST, SECOND = pl.ds(0, 192), pl.ds(0, 96), pl.ds(96, 96)

    def distance(k):
        d = lax.rem(k - z + Z, Z)
        e = jnp.where(d > 8, 1, 0)
        return jnp.where(d > 8, Z - d, d), e

    def hop(k, dist, e):
        def add(rows, wide):
            got = in32 if wide else in16
            return part[k, rows, :] + got[e, k, rows, :].astype(jnp.float32)

        @pl.when(dist == 8)
        def _():
            st16[k] = part[k].astype(jnp.bfloat16)
            chain(None, 0, k, False, FIRST).start()
            chain(None, 1, k, False, SECOND).start()

        @pl.when(dist == 7)
        def _():
            held = pl.ds(pl.multiple_of(e * 96, 96), 96)
            own = pl.ds(pl.multiple_of(96 - e * 96, 96), 96)
            chain(None, e, k, False, held).wait_recv()
            st16[k, held, :] = add(held, False).astype(jnp.bfloat16)
            st16[k, own, :] = part[k, own, :].astype(jnp.bfloat16)
            chain(None, e, k, False, ALL).start()

        @pl.when((dist < 7) & (dist > WIDE))
        def _():
            chain(None, e, k, False, ALL).wait_recv()
            st16[k] = add(ALL, False).astype(jnp.bfloat16)
            chain(None, e, k, False, ALL).start()

        @pl.when(dist == WIDE)
        def _():
            chain(None, e, k, False, ALL).wait_recv()
            st32[k] = add(ALL, False)
            chain(None, e, k, True, ALL).start()

        @pl.when((dist < WIDE) & (dist > 0))
        def _():
            chain(None, e, k, True, ALL).wait_recv()
            st32[k] = add(ALL, True)
            chain(None, e, k, True, ALL).start()

        @pl.when(dist == 0)
        def _():
            chain(None, 0, k, True, ALL).wait_recv()
            chain(None, 1, k, True, ALL).wait_recv()
            total = part[k] + in32[0, k] + in32[1, k]
            out_ref[...] = (total * row_ref[...] * col_ref[...]).astype(jnp.bfloat16)

    du_word, dv_word = packed([o[0] for o in ORDER]), packed([o[1] for o in ORDER])

    def chip_at(s):
        du = (du_word >> (2 * s)) & 3
        dv = (dv_word >> (2 * s)) & 3
        return chip(du, dv)

    def hops(s, low, high):
        def one(j, carry):
            k = chip_at(s - j)
            dist, e = distance(k)
            @pl.when(dist == 8 - j)
            def _():
                hop(k, dist, e)
            return carry
        lax.fori_loop(low, high, one, 0)

    def multiply(classes):
        def step(s, carry):
            k = chip_at(s)
            for h in range(2):
                pltpu.make_async_remote_copy(
                    src_ref=act.at[0, 0], dst_ref=act.at[2 * k + 1 - core, h], send_sem=ag_send.at[k, h, 4],
                    recv_sem=sib_recv.at[k, h], device_id={"seq": sibling}, device_id_type=MESH).wait_recv()
            rows = act[pl.ds(2 * k, 2)].reshape(192, 1792)
            part[k] = jnp.dot(rows, w_ref[...], preferred_element_type=jnp.float32)
            hops(s, 0, jnp.minimum(s, 8) + 1)
            return carry
        lax.fori_loop(CLASS[classes][0], CLASS[classes][-1] + 1, step, 0)

    for h in range(2):
        run(0, 0, h, "start")
    receive(1)
    multiply(0)
    receive(2)
    multiply(1)
    receive(3)
    multiply(2)
    receive(4)
    multiply(3)
    multiply(4)

    def drain(s, carry):
        hops(s, s - 15, 9)
        return carry
    lax.fori_loop(16, 24, drain, 0)

    for h in range(2):
        for du, dv in ORDER:
            run(du, dv, h, "wait_send")

    def settle(k, carry):
        dist, e = distance(k)
        @pl.when(dist == 8)
        def _():
            chain(None, 0, k, False, FIRST).wait_send()
            chain(None, 1, k, False, SECOND).wait_send()
        @pl.when((dist < 8) & (dist > WIDE))
        def _():
            chain(None, e, k, False, ALL).wait_send()
        @pl.when((dist <= WIDE) & (dist > 0))
        def _():
            chain(None, e, k, True, ALL).wait_send()
        return carry
    lax.fori_loop(0, Z, settle, 0)


def project(q, w, row_scale, col_scale):
    v = pl.BlockSpec(memory_space=pltpu.VMEM)
    dma = pltpu.SemaphoreType.DMA
    bf, f32 = jnp.bfloat16, jnp.float32
    return pl.pallas_call(
        k2, out_shape=jax.ShapeDtypeStruct((192, 256), bf),
        in_specs=[v] * 4, out_specs=v,
        scratch_shapes=[
            pltpu.VMEM((32, 2, 48, 1792), bf), pltpu.VMEM((16, 192, 256), f32),
            pltpu.VMEM((2, 16, 192, 256), bf), pltpu.VMEM((2, 16, 192, 256), f32),
            pltpu.VMEM((16, 192, 256), bf), pltpu.VMEM((16, 192, 256), f32),
            dma((16, 2)), dma((16, 2)), dma((16, 2, 5)), dma((2, 16)), dma((2, 16))],
        compiler_params=pltpu.CompilerParams(collective_id=1, has_side_effects=True, vmem_limit_bytes=56 << 20),
    )(q, w, row_scale, col_scale)


def body(gate, up, w, exponents, ts):
    own = lax.dynamic_slice_in_dim(ts, lax.axis_index("seq") * ROWS, ROWS)
    scale = jnp.broadcast_to(((1.0 / math.sqrt(28672)) / own)[:, None], (ROWS, 128))
    q = rotate(gate, up, scale)
    row = lax.dynamic_slice_in_dim(ts, lax.axis_index("tp") * 192, 192)[:, None]
    return project(q, w, row, jnp.exp2(exponents.astype(jnp.float32))[None, :])


def solution(mesh):
    placed = (P("seq", "tp"), P("seq", "tp"), P("tp", "seq"), P("seq"), P())
    return jax.shard_map(body, mesh=mesh, in_specs=placed, out_specs=P("tp", "seq"), check_vma=False)
```

```python
import math

import jax
import jax.numpy as jnp
import numpy as np
from jax import lax
from jax.experimental import pallas as pl
from jax.experimental.pallas import tpu as pltpu
from jax.sharding import PartitionSpec as P

MESH = pl.DeviceIdType.MESH
Z = 16
TILES = 14
ROWS = 96
WIDTH = 1792
COLS = 256
SIZES = (16, 16, 16, 16, 16, 16)
OFFS = tuple(sum(SIZES[:i]) for i in range(len(SIZES)))
CHUNKS = len(SIZES)
DIRECT = (False, False, False, False, False, False)
FAR = (8, 7, 9, 6, 10, 5, 11, 4, 12, 3, 13, 2, 14, 1, 15)
TREES = ((0, 2, 0, 2, 2, 6, 0, 6, 6, 11, 11, 0, 11, 14, 0, 14),
         (0, 0, 3, 0, 3, 6, 3, 6, 6, 11, 11, 14, 11, 14, 0, 14),
         (0, 0, 0, 2, 2, 4, 4, 6, 6, 10, 12, 12, 14, 14, 0, 0))
TREE = (0, 0, 0, 0, 0, 0)
BLOCKS = ((1, 0), (3, 0), (2, 0), (0, 1), (0, 3), (1, 1), (1, 3), (3, 1), (3, 3), (2, 1), (2, 3), (0, 2), (1, 2), (3, 2),
          (2, 2))
GROUPS = (0, 1, 3, 2)
SCHED = (
    "R0", "A0", "R1", "A1", "R2", "R3", "R4", "R5", "S0", "A2", "S1", "A3", "G0", "S2", "A4", "E0.2", "G1",
    "E0.0", "E0.1", "E0.3", "E0.4", "S3", "A5", "E0.9", "E0.10", "G2", "E1.2", "E1.0", "E1.1", "E1.3", "E1.4",
    "E0.5", "E0.6", "E0.7", "E0.8", "S4", "E0.11", "M0.01", "E0.14", "E2.2", "G3", "E2.0", "E2.1", "E2.3",
    "E2.4", "E1.9", "E1.10", "E1.5", "E1.6", "E1.7", "S5", "E0.12", "E0.13", "E1.8", "E1.11", "M0.12", "E2.9",
    "M0.23", "G4", "E2.10", "E3.2", "E3.0", "E3.1", "M0.34", "E3.3", "E2.5", "E3.4", "E2.6", "M1.01", "E2.7",
    "E2.8", "E2.11", "M2.01", "E1.14", "E1.12", "E1.13", "M1.12", "E2.14", "M1.23", "G5", "E4.2", "E4.0",
    "E4.1", "M1.34", "E4.3", "E3.9", "E4.4", "E3.10", "H0.2", "E3.5", "H0.6", "E3.6", "H0.11", "E3.7", "H0.14",
    "E3.8", "E3.11", "M3.01", "E2.12", "E2.13", "M2.13", "E5.2", "E5.0", "E5.1", "E5.3", "M2.34", "E4.9",
    "E5.4", "E4.10", "H1.2", "E4.5", "H1.6", "E4.6", "E4.7", "H1.11", "E4.8", "H1.14", "E4.11", "M4.01",
    "E3.14", "E3.12", "E3.13", "K0", "M3.12", "E5.9", "E5.10", "E5.5", "E5.6", "M3.23", "E5.7", "E5.8", "E5.11",
    "H2.2", "E4.14", "E4.12", "H2.6", "E4.13", "H2.11", "H2.14", "M3.34", "M4.13", "K1", "E5.14", "M4.34",
    "E5.12", "M5.01", "E5.13", "M5.14", "K2", "H3.2", "H3.6", "H3.11", "H3.14", "H4.2", "H4.6", "H4.11",
    "H4.14", "H5.2", "H5.6", "H5.11", "H5.14", "K3", "K4", "K5",
)


def paley_table():
    residues = [number * number % 13 for number in range(1, 13)]
    legendre = np.array([0.0] + [1.0 if number in residues else -1.0 for number in range(1, 13)])
    offsets = (np.arange(13)[None, :] - np.arange(13)[:, None]) % 13
    conference = np.zeros((14, 14))
    conference[0, 1:] = 1.0
    conference[1:, 0] = 1.0
    conference[1:, 1:] = legendre[offsets]
    upper_pair = np.array([[1.0, 1.0], [1.0, -1.0]])
    lower_pair = np.array([[1.0, -1.0], [-1.0, -1.0]])
    return np.kron(conference, upper_pair) + np.kron(np.eye(14), lower_pair)


def sylvester(order):
    table = np.ones((1, 1))
    doubling = np.array([[1.0, 1.0], [1.0, -1.0]])
    for _ in range(order.bit_length() - 1):
        table = np.kron(doubling, table)
    return table


def kernel(gate_hbm, up_hbm, w_hbm, mix_hbm, ts_ref, exp_ref, out_ref,
           gate, up, w, mix, send_buf, recv_buf, q_buf, act, part, staged, landed, scale_ref,
           in_sem, a1_send, a1_recv, a2_send, a2_recv, ag_send, ag_recv, sib_recv, rs_send, rs_recv):
    f32, bf16 = jnp.float32, jnp.bfloat16
    z = lax.axis_index("tp")
    seq = lax.axis_index("seq")
    core = lax.rem(seq, 2)
    x, y = seq // 8, lax.rem(seq // 2, 4)
    u = x * (1 - core) + y * core
    v = y * (1 - core) + x * core
    sibling = seq + 1 - 2 * core

    def place(uu, vv):
        return 8 * (uu * (1 - core) + vv * core) + 2 * (vv * (1 - core) + uu * core) + core

    def at_u(d):
        return place(lax.rem(u + d, 4), v)

    def at_v(d):
        return place(u, lax.rem(v + d, 4))

    def at_z(d):
        return lax.rem(z + d, Z)

    loads = [pltpu.make_async_copy(src, dst, in_sem.at[i])
             for i, (src, dst) in enumerate(((gate_hbm, gate), (up_hbm, up), (mix_hbm, mix), (w_hbm, w)))]
    for load in loads:
        load.start()

    barrier = pltpu.get_barrier_semaphore()
    for d in FAR:
        pl.semaphore_signal(barrier, inc=1, device_id={"tp": at_z(d)}, device_id_type=MESH)
    for d in (2, 1, 3):
        pl.semaphore_signal(barrier, inc=1, device_id={"seq": at_u(d)}, device_id_type=MESH)
        pl.semaphore_signal(barrier, inc=1, device_id={"seq": at_v(d)}, device_id_type=MESH)
    pl.semaphore_signal(barrier, inc=1, device_id={"seq": sibling}, device_id_type=MESH)

    def column(first, count):
        tokens = lax.broadcasted_iota(jnp.int32, (count, 3072), 1)
        wanted = lax.broadcasted_iota(jnp.int32, (count, 3072), 0) + first
        return jnp.sum(jnp.where(tokens == wanted, ts_ref[...], 0.0), axis=1, keepdims=True)

    scale_ref[...] = jnp.broadcast_to((1.0 / math.sqrt(28672)) / column(ROWS * seq, ROWS), (ROWS, 128))

    def rows_of(i):
        return pl.ds(OFFS[i], SIZES[i])

    def pairs_of(i):
        return pl.ds(2 * OFFS[i], 2 * SIZES[i])

    shift = 8 * core
    mine = lax.rem(z + Z - shift, Z)

    def mix_rows(i):
        n, rows = SIZES[i], rows_of(i)
        g = gate[rows, :].astype(f32)
        hidden = g / (1.0 + jnp.exp(-g)) * up[rows, :].astype(f32)
        hi = hidden.astype(bf16)
        lo = (hidden - hi.astype(f32)).astype(bf16)
        half = WIDTH // 2
        stacked = jnp.concatenate([hi[:, :half], hi[:, half:], lo[:, :half], lo[:, half:]], axis=0)
        mixed = jnp.dot(stacked, mix[...], preferred_element_type=f32)
        first = mixed[:n] + mixed[2 * n:3 * n]
        second = mixed[n:2 * n] + mixed[3 * n:]
        plus = (first + second).astype(bf16)
        minus = (first - second).astype(bf16)
        for t in range(TILES // 2):
            send_buf[t, rows, :] = plus[:, t * 128:(t + 1) * 128]
            send_buf[TILES // 2 + t, rows, :] = minus[:, t * 128:(t + 1) * 128]

    def to_combiner(i, tile, slot, dest):
        return pltpu.make_async_remote_copy(
            src_ref=send_buf.at[tile, rows_of(i)], dst_ref=recv_buf.at[slot, rows_of(i)], send_sem=a1_send.at[i],
            recv_sem=a1_recv.at[i], device_id={"tp": dest}, device_id_type=MESH)

    def send_tiles(i):
        for d in FAR:
            dest = at_z(d)
            tile = lax.rem(dest + Z - shift, Z)
            @pl.when(tile < TILES)
            def _():
                to_combiner(i, tile, z, dest).start()

    def bytes_of(buf, count, rows, send_sem, recv_sem, what):
        copy = pltpu.make_async_remote_copy(
            src_ref=buf.at[pl.ds(0, count), rows], dst_ref=buf.at[pl.ds(0, count), rows], send_sem=send_sem,
            recv_sem=recv_sem, device_id={"tp": at_z(1)}, device_id_type=MESH)
        getattr(copy, what)()

    def from_combiner(i, dest):
        lanes = pl.ds(pl.multiple_of(mine * 128, 128), 128)
        return pltpu.make_async_remote_copy(
            src_ref=q_buf.at[dest, rows_of(i)], dst_ref=act.at[seq, rows_of(i), lanes],
            send_sem=a2_send.at[i], recv_sem=a2_recv.at[i], device_id={"tp": dest}, device_id_type=MESH)

    def combine(i):
        @pl.when(mine < TILES)
        def _():
            recv_buf[z, rows_of(i), :] = send_buf[mine, rows_of(i), :]
            bytes_of(recv_buf, Z - 1, rows_of(i), a1_send.at[i], a1_recv.at[i], "wait_recv")

            def some(r, carry):
                rows = pl.ds(pl.multiple_of(OFFS[i] + r * 16, 16), 16)
                held = [recv_buf[j, rows, :].astype(f32) for j in range(Z)]
                step = 1
                while step < Z:
                    held = [held[j] + held[j | step] if j & step == 0 else held[j ^ step] - held[j]
                            for j in range(Z)]
                    step *= 2
                factor = scale_ref[rows, :]
                for j in range(Z):
                    q_buf[j, rows, :] = jnp.clip(held[j] * factor, -127.0, 127.0).astype(bf16)
                return carry

            lax.fori_loop(0, SIZES[i] // 16, some, 0)
            for d in FAR:
                from_combiner(i, at_z(d)).start()
            act[seq, rows_of(i), pl.ds(pl.multiple_of(mine * 128, 128), 128)] = q_buf[z, rows_of(i), :]

    def along(block, i, peer):
        return pltpu.make_async_remote_copy(
            src_ref=act.at[block, rows_of(i)], dst_ref=act.at[block, rows_of(i)], send_sem=ag_send.at[i],
            recv_sem=ag_recv.at[i, block // 2], device_id={"seq": peer}, device_id_type=MESH)

    def to_sibling(block, i):
        return pltpu.make_async_remote_copy(
            src_ref=act.at[block, rows_of(i)], dst_ref=act.at[block, rows_of(i)], send_sem=ag_send.at[i],
            recv_sem=sib_recv.at[i, block // 8], device_id={"seq": sibling}, device_id_type=MESH)

    def pass_on(i, du, dv):
        bu, bv = lax.rem(u + du, 4), lax.rem(v + dv, 4)
        block = place(bu, bv)
        if dv == 0:
            if du == 0:
                for d in (2, 1, 3):
                    along(block, i, at_u(d)).start()
            for d in ((2, 1, 3) if DIRECT[i] else (1, 3)):
                along(block, i, at_v(d)).start()
        elif dv != 2 and not DIRECT[i]:
            right = lax.rem(bu + bv + i, 2) == 0
            pl.when(right if dv == 3 else jnp.logical_not(right))(along(block, i, at_v(4 - dv)).start)
        to_sibling(block, i).start()


    def gather(i):
        have = mine < TILES
        @pl.when(have)
        def _():
            bytes_of(recv_buf, TILES - 1, rows_of(i), a2_send.at[i], a2_recv.at[i], "wait_recv")
        @pl.when(jnp.logical_not(have))
        def _():
            bytes_of(recv_buf, TILES, rows_of(i), a2_send.at[i], a2_recv.at[i], "wait_recv")
        pass_on(i, 0, 0)

    def receive(i, j):
        du, dv = BLOCKS[j]
        block = place(lax.rem(u + du, 4), lax.rem(v + dv, 4))
        along(block, i, seq).wait_recv()
        pass_on(i, du, dv)

    def children(i, pos):
        return [p for p in range(1, Z) if TREES[TREE[i]][p] == pos]

    def word(values, bits):
        total = sum(value << (bits * j) for j, value in enumerate(values))
        return total - (1 << 32) if total >= 1 << 31 else total

    def parent_of(i, pos):
        tree = TREES[TREE[i]]
        half = jnp.where(pos < 8, word(tree[:8], 4), word(tree[8:], 4))
        return (half >> (4 * lax.rem(pos, 8))) & 15

    def device_at(k, pos):
        return jnp.where(lax.rem(k, 2) == 0, lax.rem(k + pos, Z), lax.rem(k + Z - pos, Z))

    def target_at(pos):
        k = lax.rem(z + Z - pos, Z)
        return jnp.where(lax.rem(k, 2) == 0, k, lax.rem(z + pos, Z))

    def summed(i, pos, kind, dest):
        return pltpu.make_async_remote_copy(
            src_ref=staged.at[pos, pairs_of(i)], dst_ref=landed.at[pos, pairs_of(i)], send_sem=rs_send.at[i],
            recv_sem=rs_recv.at[i, kind], device_id={"tp": dest}, device_id_type=MESH)

    def multiply(i, groups):
        n = SIZES[i]
        def one(g, carry):
            dx = (sum(d << (2 * j) for j, d in enumerate(GROUPS)) >> (2 * g)) & 3
            xx = lax.rem(x + dx, 4)
            bytes_of(act, 4, rows_of(i), ag_send.at[i], sib_recv.at[i, xx], "wait_recv")
            rows = act[pl.ds(8 * xx, 8), rows_of(i), :].reshape(8 * n, WIDTH)
            product = jnp.dot(rows, w[...], preferred_element_type=f32)
            for j in range(4):
                k = 4 * xx + j
                mine_of = product[j * 2 * n:(j + 1) * 2 * n]
                p = lax.rem(z + Z - k, Z)
                pos = jnp.where(lax.rem(k, 2) == 0, p, lax.rem(Z - p, Z))
                parent = parent_of(i, pos)
                part[k, pairs_of(i), :] = mine_of
                staged[pos, pairs_of(i), :] = mine_of.astype(bf16)
                leaves = word([p > 0 and not children(i, p) for p in range(Z)], 1)
                @pl.when(((leaves >> pos) & 1) == 1)
                def _():
                    summed(i, pos, parent, device_at(k, parent)).start()
            return carry
        lax.fori_loop(groups[0], groups[1], one, 0)

    def collect(i, pos):
        below, parent = children(i, pos), TREES[TREE[i]][pos]
        bytes_of(landed, len(below), pairs_of(i), rs_send.at[i], rs_recv.at[i, pos], "wait_recv")
        k = target_at(pos)
        total = part[k, pairs_of(i), :]
        for child in below:
            total = total + landed[child, pairs_of(i), :].astype(f32)
        staged[pos, pairs_of(i), :] = total.astype(bf16)
        summed(i, pos, parent, device_at(k, parent)).start()

    def finish(i):
        n = SIZES[i]
        below = children(i, 0)
        bytes_of(landed, len(below), pairs_of(i), rs_send.at[i], rs_recv.at[i, 0], "wait_recv")
        total = part[z, pairs_of(i), :]
        for pos in below:
            total = total + landed[pos, pairs_of(i), :].astype(f32)
        total = total * columns
        for c in range(2):
            rows = column(192 * z + ROWS * c + OFFS[i], n)
            out_ref[pl.ds(ROWS * c + OFFS[i], n), :] = (total[c * n:(c + 1) * n] * rows).astype(bf16)

    columns = jnp.exp2(exp_ref[...].astype(f32))
    started, weights = False, False
    for task in SCHED:
        name, i = task[0], int(task[1])
        rest = int(task[3:] or 0)
        if name == "R":
            if not started:
                for load in loads[:3]:
                    load.wait()
            mix_rows(i)
            if not started:
                pl.semaphore_wait(barrier, Z - 1 + 3 + 3 + 1)
            started = True
        elif name == "A":
            send_tiles(i)
        elif name == "S":
            combine(i)
        elif name == "G":
            gather(i)
        elif name == "E":
            receive(i, rest)
        elif name == "M":
            if not weights:
                loads[3].wait()
            weights = True
            multiply(i, (rest // 10, rest % 10))
        elif name == "H":
            collect(i, rest)
        elif name == "K":
            finish(i)

    for i in range(CHUNKS):
        bytes_of(act, 31, rows_of(i), ag_send.at[i], ag_recv.at[i, 0], "wait_send")
        bytes_of(staged, 15, pairs_of(i), rs_send.at[i], rs_recv.at[i, 0], "wait_send")
        @pl.when(mine < TILES)
        def _():
            bytes_of(send_buf, TILES - 1, rows_of(i), a1_send.at[i], a1_recv.at[i], "wait_send")
            bytes_of(recv_buf, Z - 1, rows_of(i), a2_send.at[i], a2_recv.at[i], "wait_send")
        @pl.when(mine >= TILES)
        def _():
            bytes_of(send_buf, TILES, rows_of(i), a1_send.at[i], a1_recv.at[i], "wait_send")


def body(gate, up, weight_codes, exponents, token_scale):
    bf16, f32 = jnp.bfloat16, jnp.float32
    mix = jnp.asarray(np.kron(sylvester(32), paley_table()).T, bf16)
    vmem, hbm = pl.BlockSpec(memory_space=pltpu.VMEM), pl.BlockSpec(memory_space=pl.ANY)
    dma = pltpu.SemaphoreType.DMA
    tiles = pltpu.VMEM((Z, ROWS, 128), bf16)
    return pl.pallas_call(
        kernel,
        out_shape=jax.ShapeDtypeStruct((2 * ROWS, COLS), bf16),
        in_specs=[hbm] * 4 + [vmem] * 2,
        out_specs=vmem,
        scratch_shapes=[
            pltpu.VMEM((ROWS, WIDTH), bf16), pltpu.VMEM((ROWS, WIDTH), bf16), pltpu.VMEM((WIDTH, COLS), bf16),
            pltpu.VMEM((WIDTH // 2, WIDTH // 2), bf16), tiles, tiles, tiles,
            pltpu.VMEM((32, ROWS, WIDTH), bf16), pltpu.VMEM((Z, 2 * ROWS, COLS), f32),
            pltpu.VMEM((Z, 2 * ROWS, COLS), bf16), pltpu.VMEM((Z, 2 * ROWS, COLS), bf16),
            pltpu.VMEM((ROWS, 128), f32),
            dma((4,)), dma((CHUNKS,)), dma((CHUNKS,)), dma((CHUNKS,)), dma((CHUNKS,)),
            dma((CHUNKS,)), dma((CHUNKS, 16)), dma((CHUNKS, 4)), dma((CHUNKS,)), dma((CHUNKS, Z))],
        compiler_params=pltpu.CompilerParams(collective_id=0, has_side_effects=True, vmem_limit_bytes=56 << 20),
    )(gate, up, weight_codes, mix, token_scale.reshape(1, -1), exponents.reshape(1, -1))


def solution(mesh):
    placed = (P("seq", "tp"), P("seq", "tp"), P("tp", "seq"), P("seq"), P())
    return jax.shard_map(
        body, mesh=mesh, in_specs=placed, out_specs=P("tp", "seq"), check_vma=False
    )
```

```python
import math

import jax
import jax.numpy as jnp
import numpy as np
from jax import lax
from jax.experimental import pallas as pl
from jax.experimental.pallas import tpu as pltpu
from jax.sharding import PartitionSpec as P

MESH = pl.DeviceIdType.MESH
Z = 16
TILES = 14
ROWS = 96
WIDTH = 1792
COLS = 256
SIZES = (16, 16, 16, 16, 16, 16)
OFFS = tuple(sum(SIZES[:i]) for i in range(len(SIZES)))
CHUNKS = len(SIZES)
DIRECT = (False, False, False, False, False, False)
FAR = (8, 7, 9, 6, 10, 5, 11, 4, 12, 3, 13, 2, 14, 1, 15)
TREES = ((0, 2, 0, 2, 2, 6, 0, 6, 6, 11, 11, 0, 11, 14, 0, 14),
         (0, 0, 3, 0, 3, 6, 3, 6, 6, 11, 11, 14, 11, 14, 0, 14),
         (0, 0, 0, 2, 2, 4, 4, 6, 6, 10, 12, 12, 14, 14, 0, 0))
TREE = (0, 0, 0, 0, 0, 0)
BLOCKS = ((1, 0), (3, 0), (2, 0), (0, 1), (0, 3), (1, 1), (1, 3), (3, 1), (3, 3), (2, 1), (2, 3), (0, 2), (1, 2), (3, 2),
          (2, 2))
GROUPS = (0, 1, 3, 2)
SCHED = (
    "R0", "A0", "R1", "A1", "R2", "R3", "R4", "R5", "S0", "A2", "S1", "A3", "G0", "S2", "A4", "G1", "E0.2",
    "E0.0", "E0.1", "E0.3", "E0.4", "S3", "A5", "E1.2", "G2", "E1.0", "E1.1", "E1.3", "E1.4", "E0.9", "E0.10",
    "E0.5", "E0.6", "E0.7", "S4", "E0.8", "E0.11", "M0.01", "G3", "E1.9", "E1.10", "E2.2", "E2.0", "E2.1",
    "E2.3", "E2.4", "S5", "E1.5", "E1.6", "E1.7", "E1.8", "E1.11", "M1.01", "E0.14", "E0.12", "E0.13", "M0.13",
    "G4", "E3.2", "E3.0", "E3.1", "E3.3", "M0.34", "E1.14", "E3.4", "E2.9", "E2.10", "E2.5", "E2.6", "E2.7",
    "E2.8", "E2.11", "M2.01", "E1.12", "E1.13", "M1.13", "G5", "E4.2", "M1.34", "E4.0", "E4.1", "E4.3", "E4.4",
    "E3.9", "H0.2", "E3.10", "H0.6", "E3.5", "H0.11", "E3.6", "H0.14", "E3.7", "E3.8", "E3.11", "M3.01",
    "E2.14", "E2.12", "E2.13", "M2.13", "E5.2", "E5.0", "E5.1", "M2.34", "E5.3", "E4.9", "E5.4", "E4.10",
    "H1.2", "E4.5", "H1.6", "E4.6", "H1.11", "E4.7", "E4.8", "H1.14", "E4.11", "M4.01", "E3.14", "E3.12",
    "E3.13", "M3.12", "K0", "M3.23", "E5.9", "E5.10", "E5.5", "M3.34", "E5.6", "E5.7", "E5.8", "H2.2", "E5.11",
    "H2.6", "E4.14", "E4.12", "H2.11", "H2.14", "E4.13", "M4.13", "M5.01", "K1", "M4.34", "E5.14", "E5.12",
    "M5.12", "E5.13", "H3.2", "H3.6", "H3.11", "H3.14", "M5.24", "K2", "H4.2", "H4.6", "H4.11", "H4.14", "K3",
    "H5.2", "H5.6", "H5.11", "H5.14", "K4", "K5",
)


def paley_table():
    residues = [number * number % 13 for number in range(1, 13)]
    legendre = np.array([0.0] + [1.0 if number in residues else -1.0 for number in range(1, 13)])
    offsets = (np.arange(13)[None, :] - np.arange(13)[:, None]) % 13
    conference = np.zeros((14, 14))
    conference[0, 1:] = 1.0
    conference[1:, 0] = 1.0
    conference[1:, 1:] = legendre[offsets]
    upper_pair = np.array([[1.0, 1.0], [1.0, -1.0]])
    lower_pair = np.array([[1.0, -1.0], [-1.0, -1.0]])
    return np.kron(conference, upper_pair) + np.kron(np.eye(14), lower_pair)


def sylvester(order):
    table = np.ones((1, 1))
    doubling = np.array([[1.0, 1.0], [1.0, -1.0]])
    for _ in range(order.bit_length() - 1):
        table = np.kron(doubling, table)
    return table


def kernel(gate_hbm, up_hbm, w_hbm, mix_hbm, ts_ref, exp_ref, out_ref,
           gate, up, w, mix, send_buf, recv_buf, q_buf, act, part, staged, landed, scale_ref,
           in_sem, a1_send, a1_recv, a2_send, a2_recv, ag_send, ag_recv, sib_recv, rs_send, rs_recv):
    f32, bf16 = jnp.float32, jnp.bfloat16
    z = lax.axis_index("tp")
    seq = lax.axis_index("seq")
    core = lax.rem(seq, 2)
    x, y = seq // 8, lax.rem(seq // 2, 4)
    u = x * (1 - core) + y * core
    v = y * (1 - core) + x * core
    sibling = seq + 1 - 2 * core

    def place(uu, vv):
        return 8 * (uu * (1 - core) + vv * core) + 2 * (vv * (1 - core) + uu * core) + core

    def at_u(d):
        return place(lax.rem(u + d, 4), v)

    def at_v(d):
        return place(u, lax.rem(v + d, 4))

    def at_z(d):
        return lax.rem(z + d, Z)

    loads = [pltpu.make_async_copy(src, dst, in_sem.at[i])
             for i, (src, dst) in enumerate(((gate_hbm, gate), (up_hbm, up), (mix_hbm, mix), (w_hbm, w)))]
    for load in loads:
        load.start()

    barrier = pltpu.get_barrier_semaphore()
    for d in FAR:
        pl.semaphore_signal(barrier, inc=1, device_id={"tp": at_z(d)}, device_id_type=MESH)
    for d in (2, 1, 3):
        pl.semaphore_signal(barrier, inc=1, device_id={"seq": at_u(d)}, device_id_type=MESH)
        pl.semaphore_signal(barrier, inc=1, device_id={"seq": at_v(d)}, device_id_type=MESH)
    pl.semaphore_signal(barrier, inc=1, device_id={"seq": sibling}, device_id_type=MESH)

    def column(first, count):
        tokens = lax.broadcasted_iota(jnp.int32, (count, 3072), 1)
        wanted = lax.broadcasted_iota(jnp.int32, (count, 3072), 0) + first
        return jnp.sum(jnp.where(tokens == wanted, ts_ref[...], 0.0), axis=1, keepdims=True)

    scale_ref[...] = jnp.broadcast_to((1.0 / math.sqrt(28672)) / column(ROWS * seq, ROWS), (ROWS, 128))

    def rows_of(i):
        return pl.ds(OFFS[i], SIZES[i])

    def pairs_of(i):
        return pl.ds(2 * OFFS[i], 2 * SIZES[i])

    shift = 8 * core
    mine = lax.rem(z + Z - shift, Z)

    def mix_rows(i):
        n, rows = SIZES[i], rows_of(i)
        g = gate[rows, :].astype(f32)
        hidden = g / (1.0 + jnp.exp(-g)) * up[rows, :].astype(f32)
        hi = hidden.astype(bf16)
        lo = (hidden - hi.astype(f32)).astype(bf16)
        half = WIDTH // 2
        stacked = jnp.concatenate([hi[:, :half], hi[:, half:], lo[:, :half], lo[:, half:]], axis=0)
        mixed = jnp.dot(stacked, mix[...], preferred_element_type=f32)
        first = mixed[:n] + mixed[2 * n:3 * n]
        second = mixed[n:2 * n] + mixed[3 * n:]
        plus = (first + second).astype(bf16)
        minus = (first - second).astype(bf16)
        for t in range(TILES // 2):
            send_buf[t, rows, :] = plus[:, t * 128:(t + 1) * 128]
            send_buf[TILES // 2 + t, rows, :] = minus[:, t * 128:(t + 1) * 128]

    def to_combiner(i, tile, slot, dest):
        return pltpu.make_async_remote_copy(
            src_ref=send_buf.at[tile, rows_of(i)], dst_ref=recv_buf.at[slot, rows_of(i)], send_sem=a1_send.at[i],
            recv_sem=a1_recv.at[i], device_id={"tp": dest}, device_id_type=MESH)

    def send_tiles(i):
        for d in FAR:
            dest = at_z(d)
            tile = lax.rem(dest + Z - shift, Z)
            @pl.when(tile < TILES)
            def _():
                to_combiner(i, tile, z, dest).start()

    def bytes_of(buf, count, rows, send_sem, recv_sem, what):
        copy = pltpu.make_async_remote_copy(
            src_ref=buf.at[pl.ds(0, count), rows], dst_ref=buf.at[pl.ds(0, count), rows], send_sem=send_sem,
            recv_sem=recv_sem, device_id={"tp": at_z(1)}, device_id_type=MESH)
        getattr(copy, what)()

    def from_combiner(i, dest):
        lanes = pl.ds(pl.multiple_of(mine * 128, 128), 128)
        return pltpu.make_async_remote_copy(
            src_ref=q_buf.at[dest, rows_of(i)], dst_ref=act.at[seq, rows_of(i), lanes],
            send_sem=a2_send.at[i], recv_sem=a2_recv.at[i], device_id={"tp": dest}, device_id_type=MESH)

    def combine(i):
        @pl.when(mine < TILES)
        def _():
            recv_buf[z, rows_of(i), :] = send_buf[mine, rows_of(i), :]
            bytes_of(recv_buf, Z - 1, rows_of(i), a1_send.at[i], a1_recv.at[i], "wait_recv")

            def some(r, carry):
                rows = pl.ds(pl.multiple_of(OFFS[i] + r * 16, 16), 16)
                held = [recv_buf[j, rows, :].astype(f32) for j in range(Z)]
                step = 1
                while step < Z:
                    held = [held[j] + held[j | step] if j & step == 0 else held[j ^ step] - held[j]
                            for j in range(Z)]
                    step *= 2
                factor = scale_ref[rows, :]
                for j in range(Z):
                    q_buf[j, rows, :] = jnp.clip(held[j] * factor, -127.0, 127.0).astype(bf16)
                return carry

            lax.fori_loop(0, SIZES[i] // 16, some, 0)
            for d in FAR:
                from_combiner(i, at_z(d)).start()
            act[seq, rows_of(i), pl.ds(pl.multiple_of(mine * 128, 128), 128)] = q_buf[z, rows_of(i), :]

    def along(block, i, peer):
        return pltpu.make_async_remote_copy(
            src_ref=act.at[block, rows_of(i)], dst_ref=act.at[block, rows_of(i)], send_sem=ag_send.at[i],
            recv_sem=ag_recv.at[i, block // 2], device_id={"seq": peer}, device_id_type=MESH)

    def to_sibling(block, i):
        return pltpu.make_async_remote_copy(
            src_ref=act.at[block, rows_of(i)], dst_ref=act.at[block, rows_of(i)], send_sem=ag_send.at[i],
            recv_sem=sib_recv.at[i, block // 8], device_id={"seq": sibling}, device_id_type=MESH)

    def pass_on(i, du, dv):
        bu, bv = lax.rem(u + du, 4), lax.rem(v + dv, 4)
        block = place(bu, bv)
        if dv == 0:
            if du == 0:
                for d in (2, 1, 3):
                    along(block, i, at_u(d)).start()
            for d in ((2, 1, 3) if DIRECT[i] else (1, 3)):
                along(block, i, at_v(d)).start()
        elif dv != 2 and not DIRECT[i]:
            right = lax.rem(bu + bv + i, 2) == 0
            pl.when(right if dv == 3 else jnp.logical_not(right))(along(block, i, at_v(4 - dv)).start)
        to_sibling(block, i).start()


    def gather(i):
        have = mine < TILES
        @pl.when(have)
        def _():
            bytes_of(recv_buf, TILES - 1, rows_of(i), a2_send.at[i], a2_recv.at[i], "wait_recv")
        @pl.when(jnp.logical_not(have))
        def _():
            bytes_of(recv_buf, TILES, rows_of(i), a2_send.at[i], a2_recv.at[i], "wait_recv")
        pass_on(i, 0, 0)

    def receive(i, j):
        du, dv = BLOCKS[j]
        block = place(lax.rem(u + du, 4), lax.rem(v + dv, 4))
        along(block, i, seq).wait_recv()
        pass_on(i, du, dv)

    def children(i, pos):
        return [p for p in range(1, Z) if TREES[TREE[i]][p] == pos]

    def word(values, bits):
        total = sum(value << (bits * j) for j, value in enumerate(values))
        return total - (1 << 32) if total >= 1 << 31 else total

    def parent_of(i, pos):
        tree = TREES[TREE[i]]
        half = jnp.where(pos < 8, word(tree[:8], 4), word(tree[8:], 4))
        return (half >> (4 * lax.rem(pos, 8))) & 15

    def device_at(k, pos):
        return jnp.where(lax.rem(k, 2) == 0, lax.rem(k + pos, Z), lax.rem(k + Z - pos, Z))

    def target_at(pos):
        k = lax.rem(z + Z - pos, Z)
        return jnp.where(lax.rem(k, 2) == 0, k, lax.rem(z + pos, Z))

    def summed(i, pos, kind, dest):
        return pltpu.make_async_remote_copy(
            src_ref=staged.at[pos, pairs_of(i)], dst_ref=landed.at[pos, pairs_of(i)], send_sem=rs_send.at[i],
            recv_sem=rs_recv.at[i, kind], device_id={"tp": dest}, device_id_type=MESH)

    def multiply(i, groups):
        n = SIZES[i]
        def one(g, carry):
            dx = (sum(d << (2 * j) for j, d in enumerate(GROUPS)) >> (2 * g)) & 3
            xx = lax.rem(x + dx, 4)
            bytes_of(act, 4, rows_of(i), ag_send.at[i], sib_recv.at[i, xx], "wait_recv")
            rows = act[pl.ds(8 * xx, 8), rows_of(i), :].reshape(8 * n, WIDTH)
            product = jnp.dot(rows, w[...], preferred_element_type=f32)
            for j in range(4):
                k = 4 * xx + j
                mine_of = product[j * 2 * n:(j + 1) * 2 * n]
                p = lax.rem(z + Z - k, Z)
                pos = jnp.where(lax.rem(k, 2) == 0, p, lax.rem(Z - p, Z))
                parent = parent_of(i, pos)
                part[k, pairs_of(i), :] = mine_of
                staged[pos, pairs_of(i), :] = mine_of.astype(bf16)
                leaves = word([p > 0 and not children(i, p) for p in range(Z)], 1)
                @pl.when(((leaves >> pos) & 1) == 1)
                def _():
                    summed(i, pos, parent, device_at(k, parent)).start()
            return carry
        lax.fori_loop(groups[0], groups[1], one, 0)

    def collect(i, pos):
        below, parent = children(i, pos), TREES[TREE[i]][pos]
        bytes_of(landed, len(below), pairs_of(i), rs_send.at[i], rs_recv.at[i, pos], "wait_recv")
        k = target_at(pos)
        total = part[k, pairs_of(i), :]
        for child in below:
            total = total + landed[child, pairs_of(i), :].astype(f32)
        staged[pos, pairs_of(i), :] = total.astype(bf16)
        summed(i, pos, parent, device_at(k, parent)).start()

    def finish(i):
        n = SIZES[i]
        below = children(i, 0)
        bytes_of(landed, len(below), pairs_of(i), rs_send.at[i], rs_recv.at[i, 0], "wait_recv")
        total = part[z, pairs_of(i), :]
        for pos in below:
            total = total + landed[pos, pairs_of(i), :].astype(f32)
        total = total * columns
        for c in range(2):
            rows = column(192 * z + ROWS * c + OFFS[i], n)
            out_ref[pl.ds(ROWS * c + OFFS[i], n), :] = (total[c * n:(c + 1) * n] * rows).astype(bf16)

    columns = jnp.exp2(exp_ref[...].astype(f32))
    started, weights = False, False
    for task in SCHED:
        name, i = task[0], int(task[1])
        rest = int(task[3:] or 0)
        if name == "R":
            if not started:
                for load in loads[:3]:
                    load.wait()
            mix_rows(i)
            if not started:
                pl.semaphore_wait(barrier, Z - 1 + 3 + 3 + 1)
            started = True
        elif name == "A":
            send_tiles(i)
        elif name == "S":
            combine(i)
        elif name == "G":
            gather(i)
        elif name == "E":
            receive(i, rest)
        elif name == "M":
            if not weights:
                loads[3].wait()
            weights = True
            multiply(i, (rest // 10, rest % 10))
        elif name == "H":
            collect(i, rest)
        elif name == "K":
            finish(i)

    for i in range(CHUNKS):
        bytes_of(act, 31, rows_of(i), ag_send.at[i], ag_recv.at[i, 0], "wait_send")
        bytes_of(staged, 15, pairs_of(i), rs_send.at[i], rs_recv.at[i, 0], "wait_send")
        @pl.when(mine < TILES)
        def _():
            bytes_of(send_buf, TILES - 1, rows_of(i), a1_send.at[i], a1_recv.at[i], "wait_send")
            bytes_of(recv_buf, Z - 1, rows_of(i), a2_send.at[i], a2_recv.at[i], "wait_send")
        @pl.when(mine >= TILES)
        def _():
            bytes_of(send_buf, TILES, rows_of(i), a1_send.at[i], a1_recv.at[i], "wait_send")


def body(gate, up, weight_codes, exponents, token_scale):
    bf16, f32 = jnp.bfloat16, jnp.float32
    mix = jnp.asarray(np.kron(sylvester(32), paley_table()).T, bf16)
    vmem, hbm = pl.BlockSpec(memory_space=pltpu.VMEM), pl.BlockSpec(memory_space=pl.ANY)
    dma = pltpu.SemaphoreType.DMA
    tiles = pltpu.VMEM((Z, ROWS, 128), bf16)
    return pl.pallas_call(
        kernel,
        out_shape=jax.ShapeDtypeStruct((2 * ROWS, COLS), bf16),
        in_specs=[hbm] * 4 + [vmem] * 2,
        out_specs=vmem,
        scratch_shapes=[
            pltpu.VMEM((ROWS, WIDTH), bf16), pltpu.VMEM((ROWS, WIDTH), bf16), pltpu.VMEM((WIDTH, COLS), bf16),
            pltpu.VMEM((WIDTH // 2, WIDTH // 2), bf16), tiles, tiles, tiles,
            pltpu.VMEM((32, ROWS, WIDTH), bf16), pltpu.VMEM((Z, 2 * ROWS, COLS), f32),
            pltpu.VMEM((Z, 2 * ROWS, COLS), bf16), pltpu.VMEM((Z, 2 * ROWS, COLS), bf16),
            pltpu.VMEM((ROWS, 128), f32),
            dma((4,)), dma((CHUNKS,)), dma((CHUNKS,)), dma((CHUNKS,)), dma((CHUNKS,)),
            dma((CHUNKS,)), dma((CHUNKS, 16)), dma((CHUNKS, 4)), dma((CHUNKS,)), dma((CHUNKS, Z))],
        compiler_params=pltpu.CompilerParams(collective_id=0, has_side_effects=True, vmem_limit_bytes=56 << 20),
    )(gate, up, weight_codes, mix, token_scale.reshape(1, -1), exponents.reshape(1, -1))


def solution(mesh):
    placed = (P("seq", "tp"), P("seq", "tp"), P("tp", "seq"), P("seq"), P())
    return jax.shard_map(
        body, mesh=mesh, in_specs=placed, out_specs=P("tp", "seq"), check_vma=False
    )
```
